512 devices in a mesh: row: 64 (over y, z), col: 8 (over x, core).
Axes of the slice: x: 4, y: 4, z: 16, core: 2. Of those that a mesh axis runs over, the one named last changes fastest.
Arguments:
- activations: bfloat16 [512, 8192], P('row', 'col'), may hold values from -6 to 6
- gate_weight: bfloat16 [8192, 16384], P('col', 'row'), may hold values from -0.0625 to 0.0625
- up_weight: bfloat16 [8192, 16384], P('col', 'row'), may hold values from -0.0625 to 0.0625
- down_weight: bfloat16 [16384, 8192], P('row', 'col'), may hold values from -0.046875 to 0.046875
- out_grad: bfloat16 [512, 8192], P('row', 'col'), may hold values from -2.390625 to 2.390625
Outputs:
- grad_input: float32 [512, 8192], P('row', 'col')
- grad_gate_weight: bfloat16 [8192, 16384], P('col', 'row')
- grad_up_weight: bfloat16 [8192, 16384], P('col', 'row')
- grad_down_weight: bfloat16 [16384, 8192], P('row', 'col')
The draws below stay inside these ranges and needn't reach their ends.
All inputs are finite; a program needn't handle non-finite values.
Results may differ from the reference program's by a relative error of at most 0.0049.
Values may be sent and summed in bfloat16 or wider, within the bound.
A program may use at most 64 MiB of HBM per device.

```python
import jax
import jax.numpy as jnp
from jax import lax

D = 8192
FF = 16384
TOKENS = 512


def shard_levels(own_key, dims, shards, low, largest):
    loudness, own = 1.0, jax.random.fold_in(own_key, 6)
    for position, blocks in shards:
        draws = jnp.exp(jax.random.uniform(jax.random.fold_in(own, position), (blocks,), jnp.float32, low / len(shards), largest / len(shards)))
        loudness = loudness * jnp.repeat(draws, dims[position] // blocks).reshape([-1 if axis == position else 1 for axis in range(len(dims))])
    return loudness


def bell_draw(own_key, extent, scale, reach, split=(), kind=jnp.bfloat16):
    entries = scale * jax.random.normal(own_key, extent, jnp.float32)
    if split:
        entries = entries * shard_levels(own_key, extent, split, -0.22, 0.18)
    return jnp.clip(entries, -reach, reach).astype(kind)


def setup_inputs(seed: int = 0) -> dict:
    seeds = jax.random.split(jax.random.key(seed), 6)
    return {
        "activations": bell_draw(seeds[0], (TOKENS, D), 1.0, 6.0, ((0, 64), (1, 8))),
        "gate_weight": bell_draw(seeds[1], (D, FF), D ** -0.5, 0.0625, ((0, 8), (1, 64))),
        "up_weight": bell_draw(seeds[2], (D, FF), D ** -0.5, 0.0625, ((0, 8), (1, 64))),
        "down_weight": bell_draw(seeds[3], (FF, D), FF ** -0.5, 0.046875, ((0, 64), (1, 8))),
        "out_grad": bell_draw(seeds[4], (TOKENS, D), 0.4, 2.390625, ((0, 64), (1, 8))),
    }


def reference(activations, gate_weight, up_weight, down_weight, out_grad):
    pre_gate = jnp.dot(activations, gate_weight, preferred_element_type=jnp.float32)
    pre_up = jnp.dot(activations, up_weight, preferred_element_type=jnp.float32)
    sigma = jax.nn.sigmoid(pre_gate)
    silu_gate = pre_gate * sigma
    hidden = (silu_gate * pre_up).astype(jnp.bfloat16)
    grad_hidden = lax.dot_general(out_grad, down_weight, (((1,), (1,)), ((), ())), preferred_element_type=jnp.float32)
    grad_gate = (grad_hidden * pre_up * sigma * (1.0 + pre_gate * (1.0 - sigma))).astype(jnp.bfloat16)
    grad_up = (grad_hidden * silu_gate).astype(jnp.bfloat16)
    grad_down_weight = lax.dot_general(hidden, out_grad, (((0,), (0,)), ((), ())), preferred_element_type=jnp.float32).astype(jnp.bfloat16)
    grad_gate_weight = lax.dot_general(activations, grad_gate, (((0,), (0,)), ((), ())), preferred_element_type=jnp.float32).astype(jnp.bfloat16)
    grad_up_weight = lax.dot_general(activations, grad_up, (((0,), (0,)), ((), ())), preferred_element_type=jnp.float32).astype(jnp.bfloat16)
    grad_input = lax.dot_general(grad_gate, gate_weight, (((1,), (1,)), ((), ())), preferred_element_type=jnp.float32)
    grad_input = grad_input + lax.dot_general(grad_up, up_weight, (((1,), (1,)), ((), ())), preferred_element_type=jnp.float32)
    return grad_input, grad_gate_weight, grad_up_weight, grad_down_weight
```

```python
import functools

import jax
import jax.numpy as jnp
from jax import lax
from jax.experimental import pallas as pl
from jax.experimental.pallas import tpu as pltpu
from jax.sharding import PartitionSpec as P

MESH = pl.DeviceIdType.MESH
F32, BF16 = jnp.float32, jnp.bfloat16
NY, NZ, NX, NC = 4, 16, 4, 2
TOK, HID, FEAT = 8, 256, 1024
GROUP = NY * NZ * TOK // (NX * NC)

OWN = 2


def contract_cols(left, right):
    return lax.dot_general(left, right, (((1,), (1,)), ((), ())), preferred_element_type=F32)


def contract_rows(left, right):
    return lax.dot_general(left, right, (((0,), (0,)), ((), ())), preferred_element_type=F32)


def kernel(
    x_in, wg_in, wu_in, wd_in, dy_in,
    gi_out, gw_out, uw_out, dw_out,
    xf, df, xm, dm, w2, wd,
    p2, r1, s2, r2, pd, r1d, sd, r2d,
    h_all, g_all,
    gs, yr, acc, nb, nra, nrb, nrc, cs, cr,
    gw2, dwd,
    send_sem, recv_sem, load_sem,
):
    row, col = lax.axis_index("row"), lax.axis_index("col")
    y, z = row // NZ, row % NZ
    x, c = col // NC, col % NC
    o = 1 - c

    def at(dy=0, dz=0, dx=0):
        return (
            ((y + dy + NY) % NY) * NZ + (z + dz + NZ) % NZ,
            ((x + dx + NX) % NX) * NC + c,
        )

    other = (row, x * NC + o)

    loads = []

    def load(src, dst):
        copy = pltpu.make_async_copy(src, dst, load_sem.at[len(loads)])
        copy.start()
        loads.append(copy)
        return copy

    own = [load(x_in, xf.at[0, OWN]), load(dy_in, df.at[0, OWN])]
    weights = [
        load(wg_in, w2.at[:, pl.ds(0, HID)]),
        load(wu_in, w2.at[:, pl.ds(HID, HID)]),
        load(wd_in, wd),
    ]

    peers = [at(dz=k) for k in (1, -1, 2, -2, 3, -3)]
    peers += [at(dy=k) for k in (1, -1, 2)] + [at(dx=k) for k in (1, -1, 2)] + [other]
    barrier = pltpu.get_barrier_semaphore()
    for peer in peers:
        pl.semaphore_signal(barrier, inc=1, device_id=peer, device_id_type=MESH)
    for copy in own:
        copy.wait()
    pl.semaphore_wait(barrier, len(peers))

    sent = []

    def send(src, dst, to):
        i = len(sent)
        copy = pltpu.make_async_remote_copy(
            src_ref=src, dst_ref=dst, send_sem=send_sem.at[i], recv_sem=recv_sem.at[i],
            device_id=to, device_id_type=MESH,
        )
        copy.start()
        sent.append(copy)
        return copy

    def arrived(copies):
        for copy in copies:
            copy.wait_recv()

    y_of_x = []

    def spread_y(slots):
        for k in (2, 1, 3):
            y_of_x.append(send(xf.at[0, slots], xf.at[NY - k, slots], at(dy=k)))

    def one(i):
        return pl.ds(i, 1)

    xc1 = [send(xf.at[0, one(2)], xf.at[0, one(1)], at(dz=3)), send(xf.at[0, one(2)], xf.at[0, one(3)], at(dz=-3))]
    dyy = [send(df.at[0, one(2)], df.at[NY - k, one(2)], at(dy=k)) for k in (2, 1, 3)]
    spread_y(one(2))
    arrived(xc1)
    xc2 = [send(xf.at[0, one(1)], xf.at[0, one(0)], at(dz=3)), send(xf.at[0, one(3)], xf.at[0, one(4)], at(dz=-3))]
    arrived(dyy)
    dc1 = [send(df.at[:, one(2)], df.at[:, one(1)], at(dz=3)), send(df.at[:, one(2)], df.at[:, one(3)], at(dz=-3))]
    spread_y(one(1))
    spread_y(one(3))
    arrived(xc2)
    xn = [
        send(xf.at[0, pl.ds(0, 5)], xf.at[0, pl.ds(5, 5)], at(dz=1)),
        send(xf.at[0, pl.ds(0, 5)], xf.at[0, pl.ds(10, 5)], at(dz=-1)),
        send(xf.at[0, one(4)], xf.at[0, one(15)], at(dz=-2)),
    ]
    spread_y(one(0))
    spread_y(one(4))
    arrived(dc1)
    dc2 = [send(df.at[:, one(1)], df.at[:, one(0)], at(dz=3)), send(df.at[:, one(3)], df.at[:, one(4)], at(dz=-3))]
    arrived(xn)
    spread_y(pl.ds(5, 5))
    spread_y(pl.ds(10, 5))
    spread_y(one(15))
    arrived(dc2)
    dn = [
        send(df.at[:, pl.ds(0, 5)], df.at[:, pl.ds(5, 5)], at(dz=1)),
        send(df.at[:, pl.ds(0, 5)], df.at[:, pl.ds(10, 5)], at(dz=-1)),
        send(df.at[:, one(4)], df.at[:, one(15)], at(dz=-2)),
    ]
    for copy in weights:
        copy.wait()

    def compact(src, dst):
        def body(i, carry):
            slab = src[i // 4, pl.ds((i % 4) * 4, 4)].astype(F32).reshape(4 * TOK, FEAT)
            dst[pl.ds(pl.multiple_of(i * 32, 32), 32), :] = slab.astype(BF16)
            return carry

        lax.fori_loop(0, 16, body, 0)

    def reduce_parts(tokens, weight, product, part, r1, s, r2):
        first, second = [], []
        for k in (2, 1, 3, 0):
            m = (x + k) % NX
            rows = tokens[pl.ds(pl.multiple_of(m * 2 * GROUP, 2 * GROUP), 2 * GROUP), :]
            part[m] = product(rows, weight[...]).reshape(2, GROUP, part.shape[-1])
            first.append(send(part.at[m, o], r1.at[k], other))
        for k, copy in zip((2, 1, 3, 0), first):
            copy.wait_recv()
            s[k] = part[(x + k) % NX, c] + r1[k]
            if k:
                second.append(send(s.at[k], r2.at[k], at(dx=k)))
        return second

    arrived(y_of_x)
    compact(xf, xm)
    in2 = reduce_parts(xm, w2, lambda a, b: jnp.dot(a, b, preferred_element_type=F32), p2, r1, s2, r2)
    arrived(dn)
    compact(df, dm)
    ind = reduce_parts(dm, wd, contract_cols, pd, r1d, sd, r2d)

    arrived(in2)
    pre = s2[0] + r2[1] + r2[2] + r2[3]
    pre_gate, pre_up = pre[:, :HID], pre[:, HID:]
    sigma = jax.nn.sigmoid(pre_gate)
    silu = pre_gate * sigma
    h_all[x, c] = (silu * pre_up).astype(BF16)
    hx = [send(h_all.at[x, c], h_all.at[x, c], at(dx=k)) for k in (2, 1, 3)]
    hc = [send(h_all.at[x, c], h_all.at[x, c], other)]

    arrived(ind)
    grad_hidden = sd[0] + r2d[1] + r2d[2] + r2d[3]
    g_all[x, c, :, pl.ds(0, HID)] = (grad_hidden * pre_up * sigma * (1.0 + pre_gate * (1.0 - sigma))).astype(BF16)
    g_all[x, c, :, pl.ds(HID, HID)] = (grad_hidden * silu).astype(BF16)
    gx = [send(g_all.at[x, c], g_all.at[x, c], at(dx=k)) for k in (2, 1, 3)]
    gc = [send(g_all.at[x, c], g_all.at[x, c], other)]

    def pass_on(copies, array, to_other):
        for k, copy in zip((2, 1, 3), copies):
            copy.wait_recv()
            block = array.at[(x - k + NX) % NX, c]
            to_other.append(send(block, block, other))

    pass_on(hx, h_all, hc)
    pass_on(gx, g_all, gc)
    arrived(gc)

    def input_grad(m):
        return contract_cols(g_all[m].reshape(2 * GROUP, 2 * HID), w2[...])

    ys = []
    for k in (2, 1, 3):
        gs[k] = input_grad(k).astype(BF16)
        ys.append(send(gs.at[k], yr.at[k], at(dy=k)))
    acc[...] = input_grad(0)

    outs = []
    arrived(hc)
    dwd[...] = contract_rows(h_all[...].reshape(8 * GROUP, HID), dm[...]).astype(BF16)
    outs.append(load(dwd, dw_out))
    gw2[...] = contract_rows(xm[...], g_all[...].reshape(8 * GROUP, 2 * HID)).astype(BF16)
    outs.append(load(gw2.at[:, pl.ds(0, HID)], gw_out))
    outs.append(load(gw2.at[:, pl.ds(HID, HID)], uw_out))

    arrived(ys)
    total = acc[...] + yr[1].astype(F32) + yr[2].astype(F32) + yr[3].astype(F32)
    acc[...] = total
    nb[...] = total[5 * TOK :].reshape(11, TOK, FEAT).astype(BF16)
    near = [
        send(nb.at[pl.ds(0, 5)], nra, at(dz=-1)),
        send(nb.at[pl.ds(5, 5)], nrb, at(dz=1)),
        send(nb.at[pl.ds(10, 1)], nrc, at(dz=2)),
    ]
    arrived(near)

    def slot(i):
        value = acc[pl.ds(i * TOK, TOK), :] + nra[i].astype(F32) + nrb[i].astype(F32)
        return value + nrc[0].astype(F32) if i == 4 else value

    cs[0] = slot(4).astype(BF16)
    cs[1] = slot(0).astype(BF16)
    far = [send(cs.at[0], cr.at[0], at(dz=3)), send(cs.at[1], cr.at[1], at(dz=-3))]
    arrived(far)
    cs[2] = (slot(3) + cr[0].astype(F32)).astype(BF16)
    cs[3] = (slot(1) + cr[1].astype(F32)).astype(BF16)
    last = [send(cs.at[2], cr.at[2], at(dz=3)), send(cs.at[3], cr.at[3], at(dz=-3))]
    arrived(last)
    gi_out[...] = slot(2) + cr[2].astype(F32) + cr[3].astype(F32)

    for copy in outs:
        copy.wait()
    for copy in sent:
        copy.wait_send()


N_SENDS = 80
N_LOADS = 8


def on_device(activations, gate_weight, up_weight, down_weight, out_grad):
    hbm = pl.BlockSpec(memory_space=pl.ANY)
    vmem = pl.BlockSpec(memory_space=pltpu.VMEM)
    grad_input, grad_gate, grad_up, grad_down = pl.pallas_call(
        kernel,
        out_shape=(
            jax.ShapeDtypeStruct((TOK, FEAT), F32),
            jax.ShapeDtypeStruct((FEAT, HID), BF16),
            jax.ShapeDtypeStruct((FEAT, HID), BF16),
            jax.ShapeDtypeStruct((HID, FEAT), BF16),
        ),
        in_specs=[hbm] * 5,
        out_specs=(vmem, hbm, hbm, hbm),
        scratch_shapes=[
            pltpu.VMEM((NY, NZ, TOK, FEAT), BF16),
            pltpu.VMEM((NY, NZ, TOK, FEAT), BF16),
            pltpu.VMEM((NY * NZ * TOK, FEAT), BF16),
            pltpu.VMEM((NY * NZ * TOK, FEAT), BF16),
            pltpu.VMEM((FEAT, 2 * HID), BF16),
            pltpu.VMEM((HID, FEAT), BF16),
            pltpu.VMEM((NX, NC, GROUP, 2 * HID), F32),
            pltpu.VMEM((NX, GROUP, 2 * HID), F32),
            pltpu.VMEM((NX, GROUP, 2 * HID), F32),
            pltpu.VMEM((NX, GROUP, 2 * HID), F32),
            pltpu.VMEM((NX, NC, GROUP, HID), F32),
            pltpu.VMEM((NX, GROUP, HID), F32),
            pltpu.VMEM((NX, GROUP, HID), F32),
            pltpu.VMEM((NX, GROUP, HID), F32),
            pltpu.VMEM((NX, NC, GROUP, HID), BF16),
            pltpu.VMEM((NX, NC, GROUP, 2 * HID), BF16),
            pltpu.VMEM((NY, 2 * GROUP, FEAT), BF16),
            pltpu.VMEM((NY, 2 * GROUP, FEAT), BF16),
            pltpu.VMEM((2 * GROUP, FEAT), F32),
            pltpu.VMEM((11, TOK, FEAT), BF16),
            pltpu.VMEM((5, TOK, FEAT), BF16),
            pltpu.VMEM((5, TOK, FEAT), BF16),
            pltpu.VMEM((1, TOK, FEAT), BF16),
            pltpu.VMEM((4, TOK, FEAT), BF16),
            pltpu.VMEM((4, TOK, FEAT), BF16),
            pltpu.VMEM((FEAT, 2 * HID), BF16),
            pltpu.VMEM((HID, FEAT), BF16),
            pltpu.SemaphoreType.DMA((N_SENDS,)),
            pltpu.SemaphoreType.DMA((N_SENDS,)),
            pltpu.SemaphoreType.DMA((N_LOADS,)),
        ],
        compiler_params=pltpu.CompilerParams(
            collective_id=0, has_side_effects=True, vmem_limit_bytes=48 << 20
        ),
        cost_estimate=pl.CostEstimate(
            flops=16 * NY * NZ * TOK * FEAT * HID, bytes_accessed=12 * FEAT * HID, transcendentals=0
        ),
    )(activations, gate_weight, up_weight, down_weight, out_grad)
    return grad_input, grad_gate, grad_up, grad_down


def solution(mesh):
    placed = (P("row", "col"), P("col", "row"), P("col", "row"), P("row", "col"), P("row", "col"))
    return jax.shard_map(
        on_device,
        mesh=mesh,
        in_specs=placed,
        out_specs=(P("row", "col"), P("col", "row"), P("col", "row"), P("row", "col")),
        check_vma=False,
    )
```

```python
import functools

import jax
import jax.numpy as jnp
from jax import lax
from jax.experimental import pallas as pl
from jax.experimental.pallas import tpu as pltpu
from jax.sharding import PartitionSpec as P

MESH = pl.DeviceIdType.MESH
F32, BF16 = jnp.float32, jnp.bfloat16
NY, NZ, NX, NC = 4, 16, 4, 2
TOK, HID, FEAT = 8, 256, 1024
LEFT, RIGHT = 640, 384
SLOTS = NZ // 2
GROUP = SLOTS * TOK // NC
ROWS = NY * SLOTS * TOK
WIDE = 3 * HID


def contract_cols(left, right):
    return lax.dot_general(left, right, (((1,), (1,)), ((), ())), preferred_element_type=F32)


def contract_rows(left, right):
    return lax.dot_general(left, right, (((0,), (0,)), ((), ())), preferred_element_type=F32)


def kernel(
    x_in, wg_in, wu_in, wd_in, dy_in,
    gi_out, gw_out, uw_out, dw_out,
    t, xm, dm, w2, wd,
    part, r1, s, r2, hg,
    gs, yr, acc1, acc2, nb1, nra1, nrb1, nrc1, nb2, nra2, nrb2, nrc2, ty, tr, tot, cs, cr,
    gw2, dwd,
    send_sem, recv_sem, load_sem,
):
    row, col = lax.axis_index("row"), lax.axis_index("col")
    y, z = row // NZ, row % NZ
    x, c = col // NC, col % NC
    o = 1 - c

    def at(dy=0, dz=0, dx=0):
        return (
            ((y + dy + NY) % NY) * NZ + (z + dz + NZ) % NZ,
            ((x + dx + NX) % NX) * NC + c,
        )

    other = (row, x * NC + o)

    loads = []

    def load(src, dst):
        copy = pltpu.make_async_copy(src, dst, load_sem.at[len(loads)])
        copy.start()
        loads.append(copy)
        return copy

    own = [load(x_in, t.at[0, 0, 0]), load(dy_in, t.at[1, 0, 0])]
    weights = [
        load(wg_in, w2.at[:, pl.ds(0, HID)]),
        load(wu_in, w2.at[:, pl.ds(HID, HID)]),
        load(wd_in, wd),
    ]

    peers = [at(dz=k) for k in (1, -1, 2, -2, 3, -3, 6, -6)]
    peers += [at(dy=k) for k in (1, -1, 2)] + [at(dx=k) for k in (1, -1, 2)] + [other]
    barrier = pltpu.get_barrier_semaphore()
    for peer in peers:
        pl.semaphore_signal(barrier, inc=1, device_id=peer, device_id_type=MESH)
    for copy in own:
        copy.wait()
    pl.semaphore_wait(barrier, len(peers))

    sent = []

    def send(src, dst, to):
        i = len(sent)
        copy = pltpu.make_async_remote_copy(
            src_ref=src, dst_ref=dst, send_sem=send_sem.at[i], recv_sem=recv_sem.at[i],
            device_id=to, device_id_type=MESH,
        )
        copy.start()
        sent.append(copy)
        return copy

    def arrived(copies):
        for copy in copies:
            copy.wait_recv()

    def spread(which, slots):
        return [send(t.at[which, 0, slots], t.at[which, NY - k, slots], at(dy=k)) for k in (2, 1, 3)]

    def near(which, ys, start, size):
        def to(offset):
            return t.at[which, ys, pl.ds(offset + start, size)]

        return [send(to(0), to(5), at(dz=1)), send(to(0), to(10), at(dz=-1))]

    def near_last(which, ys):
        return near(which, ys, 3, 2) + [
            send(t.at[which, ys, pl.ds(3, 1)], t.at[which, ys, pl.ds(15, 1)], at(dz=-2))
        ]

    both, acts, grads = slice(None), 0, 1
    first, all_y = pl.ds(0, 1), slice(None)
    far = []
    for i, k in ((2, 3), (1, -3)):
        far.append(send(t.at[:, 0, 0], t.at[:, 0, i], at(dz=k)))
    near0 = near(acts, first, 0, 1)
    early0 = spread(both, pl.ds(0, 1))
    arrived(near0)
    late0 = spread(acts, pl.ds(5, 1))
    late1 = spread(acts, pl.ds(10, 1))
    arrived(far[:2])
    far += [send(t.at[:, 0, 2], t.at[:, 0, 4], at(dz=3)), send(t.at[:, 0, 1], t.at[:, 0, 3], at(dz=-3))]
    near1 = near(acts, first, 1, 2)
    early1 = spread(both, pl.ds(1, 2))
    arrived(early0)
    grad_near0 = near(grads, all_y, 0, 1)
    arrived(far[2:])
    near2 = near_last(acts, first)
    early2 = spread(both, pl.ds(3, 2))
    arrived(near1)
    late0 += spread(acts, pl.ds(6, 2))
    late1 += spread(acts, pl.ds(11, 2))
    arrived(early1)
    grad_near1 = near(grads, all_y, 1, 2)
    arrived(near2)
    late1 += spread(acts, pl.ds(8, 2)) + spread(acts, pl.ds(13, 3))
    arrived(early2)
    grad_near2 = near_last(grads, all_y)
    for copy in weights:
        copy.wait()

    def compact(src, dst, half):
        for i in range(2 * NY):
            slab = t[src, i // 2, pl.ds(half * SLOTS + i % 2 * 4, 4)].astype(F32).reshape(4 * TOK, FEAT)
            dst[pl.ds(half * ROWS + i * 4 * TOK, 4 * TOK), :] = slab.astype(BF16)

    def reduce_parts(half):
        rows = pl.ds(half * ROWS, ROWS)
        compact(acts, xm, half)
        compact(grads, dm, half)
        pre = jnp.dot(xm[rows, :], w2[...], preferred_element_type=F32)
        part[half, :, :, :, pl.ds(0, 2 * HID)] = pre.reshape(NX, NC, GROUP, 2 * HID)
        part[half, :, :, :, pl.ds(2 * HID, HID)] = contract_cols(dm[rows, :], wd[...]).reshape(NX, NC, GROUP, HID)
        arrived([send(part.at[half, :, o], r1.at[half], other)])
        over_x = []
        for k in (2, 1, 3, 0):
            m = (x + k) % NX
            s[half, k] = part[half, m, c] + r1[half, m]
            if k:
                over_x.append(send(s.at[half, k], r2.at[half, k], at(dx=k)))
        return over_x

    grad_part, hid_part = pl.ds(0, 2 * HID), pl.ds(2 * HID, HID)

    def activate(half, over_x):
        arrived(over_x)
        total = s[half, 0] + r2[half, 1] + r2[half, 2] + r2[half, 3]
        pre_gate, pre_up, grad_hidden = total[:, :HID], total[:, HID : 2 * HID], total[:, 2 * HID :]
        sigma = jax.nn.sigmoid(pre_gate)
        silu = pre_gate * sigma
        grad_gate = grad_hidden * pre_up * sigma * (1.0 + pre_gate * (1.0 - sigma))
        hg[half, x, c, :, pl.ds(0, HID)] = grad_gate.astype(BF16)
        hg[half, x, c, :, pl.ds(HID, HID)] = (grad_hidden * silu).astype(BF16)
        hg[half, x, c, :, pl.ds(2 * HID, HID)] = (silu * pre_up).astype(BF16)
        mine = hg.at[half, x, c]
        return [
            [send(mine.at[:, what], mine.at[:, what], at(dx=k)) for k in (2, 1, 3)] for what in (grad_part, hid_part)
        ]

    def pass_on(half, copies, what):
        arrived(copies)
        mine = hg.at[half, :, c, :, what]
        return [send(mine, mine, other)]

    arrived(late0)
    arrived(grad_near0[:1] + grad_near1[:1])
    over_x0 = reduce_parts(0)
    arrived(late1)
    arrived(grad_near0[1:] + grad_near1[1:] + grad_near2)
    over_x1 = reduce_parts(1)
    gathered0 = activate(0, over_x0)
    gathered1 = activate(1, over_x1)
    def input_grad(half, columns):
        product = contract_cols(hg[half, :, :, :, : 2 * HID].reshape(ROWS, 2 * HID), w2[columns, :])
        return product.reshape(NY, SLOTS, TOK, product.shape[-1])

    def send_near(block, a, b, c):
        return [send(block[0], a, at(dz=-1)), send(block[1], b, at(dz=1)), send(block[2], c, at(dz=2))]

    left_y, right_near = [], []
    for half, gathered in enumerate((gathered0, gathered1)):
        arrived(pass_on(half, gathered[0], grad_part))
        rows = pl.ds(half * SLOTS * TOK, SLOTS * TOK)
        grad = input_grad(half, slice(0, LEFT)).reshape(NY, SLOTS * TOK, LEFT)
        for k in (2, 1, 3):
            gs[k, rows] = grad[k].astype(BF16)
            left_y.append(send(gs.at[k, rows], yr.at[k, rows], at(dy=k)))
        acc1[rows, :] = grad[0]
        grad = input_grad(half, slice(LEFT, FEAT))
        if half == 0:
            acc2[...] = grad[:, :5]
            nb2[:, pl.ds(0, 3)] = grad[:, 5:].astype(BF16)
            right_near.append(send(nb2.at[:, pl.ds(0, 3)], nra2.at[:, pl.ds(0, 3)], at(dz=-1)))
        else:
            nb2[:, pl.ds(3, 8)] = grad.astype(BF16)
            right_near.append(send(nb2.at[:, pl.ds(5, 5)], nrb2, at(dz=1)))
            right_near.append(send(nb2.at[:, pl.ds(3, 2)], nra2.at[:, pl.ds(3, 2)], at(dz=-1)))
            right_near.append(send(nb2.at[:, pl.ds(10, 1)], nrc2, at(dz=2)))

    outs = []
    arrived(pass_on(0, gathered0[1], hid_part) + pass_on(1, gathered1[1], hid_part))
    dwd[...] = contract_rows(hg[:, :, :, :, 2 * HID :].reshape(2 * ROWS, HID), dm[...]).astype(BF16)
    outs.append(load(dwd, dw_out))
    gw2[...] = contract_rows(xm[...], hg[:, :, :, :, : 2 * HID].reshape(2 * ROWS, 2 * HID)).astype(BF16)
    outs.append(load(gw2.at[:, pl.ds(0, HID)], gw_out))
    outs.append(load(gw2.at[:, pl.ds(HID, HID)], uw_out))

    arrived(right_near)
    right_y = []
    for k in (2, 1, 3, 0):
        acc2[k] += nra2[k].astype(F32) + nrb2[k].astype(F32)
        acc2[k, 3] += nrc2[k, 0].astype(F32)
        if k:
            ty[k] = acc2[k].astype(BF16)
            right_y.append(send(ty.at[k], tr.at[k], at(dy=k)))

    arrived(left_y)
    total = acc1[...] + yr[1].astype(F32) + yr[2].astype(F32) + yr[3].astype(F32)
    acc1[...] = total
    nb1[...] = total[5 * TOK :].reshape(11, TOK, LEFT).astype(BF16)
    left_near = send_near([nb1.at[pl.ds(0, 5)], nb1.at[pl.ds(5, 5)], nb1.at[pl.ds(10, 1)]], nra1, nrb1, nrc1)
    left, right = pl.ds(0, LEFT), pl.ds(LEFT, RIGHT)
    arrived(right_y)
    tot[:, :, right] = acc2[0] + tr[1].astype(F32) + tr[2].astype(F32) + tr[3].astype(F32)
    arrived(left_near)
    tot[:, :, left] = acc1[: 5 * TOK].reshape(5, TOK, LEFT) + nra1[...].astype(F32) + nrb1[...].astype(F32)
    tot[3, :, left] += nrc1[0].astype(F32)

    far = []
    for i, k in ((3, 6), (4, -6), (1, 3), (2, -3)):
        cs[i] = tot[i].astype(BF16)
        far.append(send(cs.at[i], cr.at[i], at(dz=k)))
    arrived(far)
    gi_out[...] = tot[0] + cr[1].astype(F32) + cr[2].astype(F32) + cr[3].astype(F32) + cr[4].astype(F32)

    for copy in outs:
        copy.wait()
    for copy in sent:
        copy.wait_send()


def write_out(*refs):
    copies = [pltpu.make_async_copy(refs[i], refs[4 + i], refs[8].at[i]) for i in range(4)]
    for copy in copies:
        copy.start()
    for copy in copies:
        copy.wait()


N_SENDS = 96
N_LOADS = 8


def on_device(activations, gate_weight, up_weight, down_weight, out_grad):
    anywhere = pl.BlockSpec(memory_space=pl.ANY)
    hbm = pl.BlockSpec(memory_space=pltpu.HBM)
    vmem = pl.BlockSpec(memory_space=pltpu.VMEM)
    results = pl.pallas_call(
        kernel,
        out_shape=(
            jax.ShapeDtypeStruct((TOK, FEAT), F32),
            jax.ShapeDtypeStruct((FEAT, HID), BF16),
            jax.ShapeDtypeStruct((FEAT, HID), BF16),
            jax.ShapeDtypeStruct((HID, FEAT), BF16),
        ),
        in_specs=[hbm] * 5,
        out_specs=(vmem, anywhere, anywhere, anywhere),
        scratch_shapes=[
            pltpu.VMEM((2, NY, NZ, TOK, FEAT), BF16),
            pltpu.VMEM((2 * ROWS, FEAT), BF16),
            pltpu.VMEM((2 * ROWS, FEAT), BF16),
            pltpu.VMEM((FEAT, 2 * HID), BF16),
            pltpu.VMEM((HID, FEAT), BF16),
            pltpu.VMEM((2, NX, NC, GROUP, WIDE), F32),
            pltpu.VMEM((2, NX, GROUP, WIDE), F32),
            pltpu.VMEM((2, NX, GROUP, WIDE), F32),
            pltpu.VMEM((2, NX, GROUP, WIDE), F32),
            pltpu.VMEM((2, NX, NC, GROUP, WIDE), BF16),
            pltpu.VMEM((NY, NZ * TOK, LEFT), BF16),
            pltpu.VMEM((NY, NZ * TOK, LEFT), BF16),
            pltpu.VMEM((NZ * TOK, LEFT), F32),
            pltpu.VMEM((NY, 5, TOK, RIGHT), F32),
            pltpu.VMEM((11, TOK, LEFT), BF16),
            pltpu.VMEM((5, TOK, LEFT), BF16),
            pltpu.VMEM((5, TOK, LEFT), BF16),
            pltpu.VMEM((1, TOK, LEFT), BF16),
            pltpu.VMEM((NY, 11, TOK, RIGHT), BF16),
            pltpu.VMEM((NY, 5, TOK, RIGHT), BF16),
            pltpu.VMEM((NY, 5, TOK, RIGHT), BF16),
            pltpu.VMEM((NY, 1, TOK, RIGHT), BF16),
            pltpu.VMEM((NY, 5, TOK, RIGHT), BF16),
            pltpu.VMEM((NY, 5, TOK, RIGHT), BF16),
            pltpu.VMEM((5, TOK, FEAT), F32),
            pltpu.VMEM((5, TOK, FEAT), BF16),
            pltpu.VMEM((5, TOK, FEAT), BF16),
            pltpu.VMEM((FEAT, 2 * HID), BF16),
            pltpu.VMEM((HID, FEAT), BF16),
            pltpu.SemaphoreType.DMA((N_SENDS,)),
            pltpu.SemaphoreType.DMA((N_SENDS,)),
            pltpu.SemaphoreType.DMA((N_LOADS,)),
        ],
        compiler_params=pltpu.CompilerParams(
            collective_id=0, has_side_effects=True, vmem_limit_bytes=62 << 20
        ),
        cost_estimate=pl.CostEstimate(
            flops=16 * NY * NZ * TOK * FEAT * HID, bytes_accessed=12 * FEAT * HID, transcendentals=0
        ),
    )(activations, gate_weight, up_weight, down_weight, out_grad)
    return pl.pallas_call(
        write_out,
        out_shape=tuple(jax.ShapeDtypeStruct(r.shape, r.dtype) for r in results),
        in_specs=[vmem] * 4,
        out_specs=(hbm,) * 4,
        scratch_shapes=[pltpu.SemaphoreType.DMA((4,))],
    )(*results)


def solution(mesh):
    placed = (P("row", "col"), P("col", "row"), P("col", "row"), P("row", "col"), P("row", "col"))
    return jax.shard_map(
        on_device,
        mesh=mesh,
        in_specs=placed,
        out_specs=(P("row", "col"), P("col", "row"), P("col", "row"), P("row", "col")),
        check_vma=False,
    )
```

```python
import functools

import jax
import jax.numpy as jnp
from jax import lax
from jax.experimental import pallas as pl
from jax.experimental.pallas import tpu as pltpu
from jax.sharding import PartitionSpec as P

MESH = pl.DeviceIdType.MESH
F32, BF16 = jnp.float32, jnp.bfloat16
NY, NZ, NX, NC = 4, 16, 4, 2
TOK, HID, FEAT = 8, 256, 1024
LEFT, RIGHT = 640, 384
SLOTS = NZ // 2
GROUP = SLOTS * TOK // NC
ROWS = NY * SLOTS * TOK
WIDE = 3 * HID


def contract_cols(left, right):
    return lax.dot_general(left, right, (((1,), (1,)), ((), ())), preferred_element_type=F32)


def contract_rows(left, right):
    return lax.dot_general(left, right, (((0,), (0,)), ((), ())), preferred_element_type=F32)


def kernel(
    x_in, wg_in, wu_in, wd_in, dy_in,
    gi_out, gw_out, uw_out, dw_out,
    t, xm, dm, w2, wd,
    part, r1, s, s16, r2, hg,
    gs, yr, acc1, acc2, nb1, nra1, nrb1, nrc1, nb2, nra2, nrb2, nrc2, ty, tr, tot, cs, cr,
    gw2, dwd,
    send_sem, recv_sem, load_sem,
):
    row, col = lax.axis_index("row"), lax.axis_index("col")
    y, z = row // NZ, row % NZ
    x, c = col // NC, col % NC
    o = 1 - c

    def at(dy=0, dz=0, dx=0):
        return (
            ((y + dy + NY) % NY) * NZ + (z + dz + NZ) % NZ,
            ((x + dx + NX) % NX) * NC + c,
        )

    other = (row, x * NC + o)

    loads = []

    def load(src, dst):
        copy = pltpu.make_async_copy(src, dst, load_sem.at[len(loads)])
        copy.start()
        loads.append(copy)
        return copy

    own = [load(x_in, t.at[0, 0, 0]), load(dy_in, t.at[1, 0, 0])]
    weights = [
        load(wg_in, w2.at[:, pl.ds(0, HID)]),
        load(wu_in, w2.at[:, pl.ds(HID, HID)]),
        load(wd_in, wd),
    ]

    peers = [at(dz=k) for k in (1, -1, 2, -2, 3, -3)]
    peers += [at(dy=k) for k in (1, -1, 2)] + [at(dx=k) for k in (1, -1, 2)] + [other]
    barrier = pltpu.get_barrier_semaphore()
    for peer in peers:
        pl.semaphore_signal(barrier, inc=1, device_id=peer, device_id_type=MESH)
    for copy in own:
        copy.wait()
    pl.semaphore_wait(barrier, len(peers))

    sent = []

    def send(src, dst, to):
        i = len(sent)
        copy = pltpu.make_async_remote_copy(
            src_ref=src, dst_ref=dst, send_sem=send_sem.at[i], recv_sem=recv_sem.at[i],
            device_id=to, device_id_type=MESH,
        )
        copy.start()
        sent.append(copy)
        return copy

    def arrived(copies):
        for copy in copies:
            copy.wait_recv()

    def spread(which, slots):
        return [send(t.at[which, 0, slots], t.at[which, NY - k, slots], at(dy=k)) for k in (2, 1, 3)]

    def near(which, ys, start, size):
        def to(offset):
            return t.at[which, ys, pl.ds(offset + start, size)]

        return [send(to(0), to(5), at(dz=1)), send(to(0), to(10), at(dz=-1))]

    def near_last(which, ys):
        return near(which, ys, 3, 2) + [
            send(t.at[which, ys, pl.ds(3, 1)], t.at[which, ys, pl.ds(15, 1)], at(dz=-2))
        ]

    both, acts, grads = slice(None), 0, 1
    first, all_y = pl.ds(0, 1), slice(None)
    far = []
    for i, k in ((2, 3), (1, -3)):
        far.append(send(t.at[:, 0, 0], t.at[:, 0, i], at(dz=k)))
    near0 = near(acts, first, 0, 1)
    early0 = spread(both, pl.ds(0, 1))
    arrived(near0)
    late0 = spread(acts, pl.ds(5, 1))
    late1 = spread(acts, pl.ds(10, 1))
    arrived(far[:2])
    far += [send(t.at[:, 0, 2], t.at[:, 0, 4], at(dz=3)), send(t.at[:, 0, 1], t.at[:, 0, 3], at(dz=-3))]
    near1 = near(acts, first, 1, 2)
    early1 = spread(both, pl.ds(1, 2))
    arrived(early0)
    grad_near0 = near(grads, all_y, 0, 1)
    arrived(far[2:])
    near2 = near_last(acts, first)
    early2 = spread(both, pl.ds(3, 2))
    arrived(near1)
    late0 += spread(acts, pl.ds(6, 2))
    late1 += spread(acts, pl.ds(11, 2))
    arrived(early1)
    grad_near1 = near(grads, all_y, 1, 2)
    arrived(near2)
    late1 += spread(acts, pl.ds(8, 2)) + spread(acts, pl.ds(13, 3))
    arrived(early2)
    grad_near2 = near_last(grads, all_y)
    for copy in weights:
        copy.wait()

    def compact(src, dst, half):
        for i in range(2 * NY):
            slab = t[src, i // 2, pl.ds(half * SLOTS + i % 2 * 4, 4)].astype(F32).reshape(4 * TOK, FEAT)
            dst[pl.ds(half * ROWS + i * 4 * TOK, 4 * TOK), :] = slab.astype(BF16)

    def reduce_parts(half):
        rows = pl.ds(half * ROWS, ROWS)
        compact(acts, xm, half)
        compact(grads, dm, half)
        pre = jnp.dot(xm[rows, :], w2[...], preferred_element_type=F32)
        part[half, :, :, :, pl.ds(0, 2 * HID)] = pre.reshape(NX, NC, GROUP, 2 * HID)
        part[half, :, :, :, pl.ds(2 * HID, HID)] = contract_cols(dm[rows, :], wd[...]).reshape(NX, NC, GROUP, HID)
        arrived([send(part.at[half, :, o], r1.at[half], other)])
        over_x = []
        for k in (2, 1, 3, 0):
            m = (x + k) % NX
            value = part[half, m, c] + r1[half, m]
            if k:
                s16[half, k] = value.astype(BF16)
                over_x.append(send(s16.at[half, k], r2.at[half, k], at(dx=k)))
            else:
                s[half] = value
        return over_x

    grad_part, hid_part = pl.ds(0, 2 * HID), pl.ds(2 * HID, HID)

    def activate(half, over_x):
        arrived(over_x)
        total = s[half] + r2[half, 1].astype(F32) + r2[half, 2].astype(F32) + r2[half, 3].astype(F32)
        pre_gate, pre_up, grad_hidden = total[:, :HID], total[:, HID : 2 * HID], total[:, 2 * HID :]
        sigma = jax.nn.sigmoid(pre_gate)
        silu = pre_gate * sigma
        grad_gate = grad_hidden * pre_up * sigma * (1.0 + pre_gate * (1.0 - sigma))
        hg[half, x, c, :, pl.ds(0, HID)] = grad_gate.astype(BF16)
        hg[half, x, c, :, pl.ds(HID, HID)] = (grad_hidden * silu).astype(BF16)
        hg[half, x, c, :, pl.ds(2 * HID, HID)] = (silu * pre_up).astype(BF16)
        mine = hg.at[half, x, c]
        return [
            [send(mine.at[:, what], mine.at[:, what], at(dx=k)) for k in (2, 1, 3)] for what in (grad_part, hid_part)
        ]

    def pass_on(half, copies, what):
        arrived(copies)
        mine = hg.at[half, :, c, :, what]
        return [send(mine, mine, other)]

    arrived(late0)
    arrived(grad_near0[:1] + grad_near1[:1])
    over_x0 = reduce_parts(0)
    arrived(late1)
    arrived(grad_near0[1:] + grad_near1[1:] + grad_near2)
    over_x1 = reduce_parts(1)
    gathered0 = activate(0, over_x0)
    gathered1 = activate(1, over_x1)
    def input_grad(half, columns):
        product = contract_cols(hg[half, :, :, :, : 2 * HID].reshape(ROWS, 2 * HID), w2[columns, :])
        return product.reshape(NY, SLOTS, TOK, product.shape[-1])

    def send_near(block, a, b, c):
        return [send(block[0], a, at(dz=-1)), send(block[1], b, at(dz=1)), send(block[2], c, at(dz=2))]

    left_y, right_near = [], []
    for half, gathered in enumerate((gathered0, gathered1)):
        arrived(pass_on(half, gathered[0], grad_part))
        rows = pl.ds(half * SLOTS * TOK, SLOTS * TOK)
        grad = input_grad(half, slice(0, LEFT)).reshape(NY, SLOTS * TOK, LEFT)
        for k in (2, 1, 3):
            gs[k, rows] = grad[k].astype(BF16)
            left_y.append(send(gs.at[k, rows], yr.at[k, rows], at(dy=k)))
        acc1[rows, :] = grad[0]
        grad = input_grad(half, slice(LEFT, FEAT))
        if half == 0:
            acc2[...] = grad[:, :5]
            nb2[:, pl.ds(0, 3)] = grad[:, 5:].astype(BF16)
            right_near.append(send(nb2.at[:, pl.ds(0, 3)], nra2.at[:, pl.ds(0, 3)], at(dz=-1)))
        else:
            nb2[:, pl.ds(3, 8)] = grad.astype(BF16)
            right_near.append(send(nb2.at[:, pl.ds(5, 5)], nrb2, at(dz=1)))
            right_near.append(send(nb2.at[:, pl.ds(3, 2)], nra2.at[:, pl.ds(3, 2)], at(dz=-1)))
            right_near.append(send(nb2.at[:, pl.ds(10, 1)], nrc2, at(dz=2)))

    outs = []
    arrived(pass_on(0, gathered0[1], hid_part) + pass_on(1, gathered1[1], hid_part))
    dwd[...] = contract_rows(hg[:, :, :, :, 2 * HID :].reshape(2 * ROWS, HID), dm[...]).astype(BF16)
    outs.append(load(dwd, dw_out))
    gw2[...] = contract_rows(xm[...], hg[:, :, :, :, : 2 * HID].reshape(2 * ROWS, 2 * HID)).astype(BF16)
    outs.append(load(gw2.at[:, pl.ds(0, HID)], gw_out))
    outs.append(load(gw2.at[:, pl.ds(HID, HID)], uw_out))

    arrived(right_near)
    right_y = []
    for k in (2, 1, 3, 0):
        acc2[k] += nra2[k].astype(F32) + nrb2[k].astype(F32)
        acc2[k, 3] += nrc2[k, 0].astype(F32)
        if k:
            ty[k] = acc2[k].astype(BF16)
            right_y.append(send(ty.at[k], tr.at[k], at(dy=k)))

    arrived(left_y)
    total = acc1[...] + yr[1].astype(F32) + yr[2].astype(F32) + yr[3].astype(F32)
    acc1[...] = total
    nb1[...] = total[5 * TOK :].reshape(11, TOK, LEFT).astype(BF16)
    left_near = send_near([nb1.at[pl.ds(0, 5)], nb1.at[pl.ds(5, 5)], nb1.at[pl.ds(10, 1)]], nra1, nrb1, nrc1)
    left, right = pl.ds(0, LEFT), pl.ds(LEFT, RIGHT)
    arrived(right_y)
    tot[:, :, right] = acc2[0] + tr[1].astype(F32) + tr[2].astype(F32) + tr[3].astype(F32)
    arrived(left_near)
    tot[:, :, left] = acc1[: 5 * TOK].reshape(5, TOK, LEFT) + nra1[...].astype(F32) + nrb1[...].astype(F32)
    tot[3, :, left] += nrc1[0].astype(F32)

    far = []
    for i, k in ((3, 6), (4, -6), (1, 3), (2, -3)):
        cs[i] = tot[i].astype(BF16)
        far.append(send(cs.at[i], cr.at[i], at(dz=k)))
    arrived(far)
    gi_out[...] = tot[0] + cr[1].astype(F32) + cr[2].astype(F32) + cr[3].astype(F32) + cr[4].astype(F32)

    for copy in outs:
        copy.wait()
    for copy in sent:
        copy.wait_send()


def write_out(*refs):
    sources, results, (small, wide, load_sem, store_sem) = refs[:4], refs[4:8], refs[8:]
    pieces = [(sources[0], small, results[0])]
    for i in range(1, 4):
        rows = sources[i].shape[0] // CHUNKS
        for j in range(CHUNKS):
            piece = pl.ds(j * rows, rows)
            held = wide[i - 1].at[piece]
            pieces.append((sources[i].at[piece], held, results[i].at[piece]))
    loads = [pltpu.make_async_copy(a, b, load_sem.at[n]) for n, (a, b, _) in enumerate(pieces)]
    stores = [pltpu.make_async_copy(b, c, store_sem.at[n]) for n, (_, b, c) in enumerate(pieces)]
    for copy in loads:
        copy.start()
    for i, copy in enumerate(loads):
        copy.wait()
        stores[i].start()
    for copy in stores:
        copy.wait()


CHUNKS = 2
N_SENDS = 96
N_LOADS = 8


def on_device(activations, gate_weight, up_weight, down_weight, out_grad):
    anywhere = pl.BlockSpec(memory_space=pl.ANY)
    hbm = pl.BlockSpec(memory_space=pltpu.HBM)
    vmem = pl.BlockSpec(memory_space=pltpu.VMEM)
    results = pl.pallas_call(
        kernel,
        out_shape=(
            jax.ShapeDtypeStruct((TOK, FEAT), F32),
            jax.ShapeDtypeStruct((FEAT, HID), BF16),
            jax.ShapeDtypeStruct((FEAT, HID), BF16),
            jax.ShapeDtypeStruct((HID, FEAT), BF16),
        ),
        in_specs=[hbm] * 5,
        out_specs=(vmem, anywhere, anywhere, anywhere),
        scratch_shapes=[
            pltpu.VMEM((2, NY, NZ, TOK, FEAT), BF16),
            pltpu.VMEM((2 * ROWS, FEAT), BF16),
            pltpu.VMEM((2 * ROWS, FEAT), BF16),
            pltpu.VMEM((FEAT, 2 * HID), BF16),
            pltpu.VMEM((HID, FEAT), BF16),
            pltpu.VMEM((2, NX, NC, GROUP, WIDE), F32),
            pltpu.VMEM((2, NX, GROUP, WIDE), F32),
            pltpu.VMEM((2, GROUP, WIDE), F32),
            pltpu.VMEM((2, NX, GROUP, WIDE), BF16),
            pltpu.VMEM((2, NX, GROUP, WIDE), BF16),
            pltpu.VMEM((2, NX, NC, GROUP, WIDE), BF16),
            pltpu.VMEM((NY, NZ * TOK, LEFT), BF16),
            pltpu.VMEM((NY, NZ * TOK, LEFT), BF16),
            pltpu.VMEM((NZ * TOK, LEFT), F32),
            pltpu.VMEM((NY, 5, TOK, RIGHT), F32),
            pltpu.VMEM((11, TOK, LEFT), BF16),
            pltpu.VMEM((5, TOK, LEFT), BF16),
            pltpu.VMEM((5, TOK, LEFT), BF16),
            pltpu.VMEM((1, TOK, LEFT), BF16),
            pltpu.VMEM((NY, 11, TOK, RIGHT), BF16),
            pltpu.VMEM((NY, 5, TOK, RIGHT), BF16),
            pltpu.VMEM((NY, 5, TOK, RIGHT), BF16),
            pltpu.VMEM((NY, 1, TOK, RIGHT), BF16),
            pltpu.VMEM((NY, 5, TOK, RIGHT), BF16),
            pltpu.VMEM((NY, 5, TOK, RIGHT), BF16),
            pltpu.VMEM((5, TOK, FEAT), F32),
            pltpu.VMEM((5, TOK, FEAT), BF16),
            pltpu.VMEM((5, TOK, FEAT), BF16),
            pltpu.VMEM((FEAT, 2 * HID), BF16),
            pltpu.VMEM((HID, FEAT), BF16),
            pltpu.SemaphoreType.DMA((N_SENDS,)),
            pltpu.SemaphoreType.DMA((N_SENDS,)),
            pltpu.SemaphoreType.DMA((N_LOADS,)),
        ],
        compiler_params=pltpu.CompilerParams(
            collective_id=0, has_side_effects=True, vmem_limit_bytes=62 << 20
        ),
        cost_estimate=pl.CostEstimate(
            flops=16 * NY * NZ * TOK * FEAT * HID, bytes_accessed=12 * FEAT * HID, transcendentals=0
        ),
    )(activations, gate_weight, up_weight, down_weight, out_grad)
    return pl.pallas_call(
        write_out,
        out_shape=tuple(jax.ShapeDtypeStruct(r.shape, r.dtype) for r in results),
        in_specs=[hbm] * 4,
        out_specs=(hbm,) * 4,
        scratch_shapes=[
            pltpu.VMEM((TOK, FEAT), F32),
            [pltpu.VMEM(r.shape, BF16) for r in results[1:]],
            pltpu.SemaphoreType.DMA((1 + 3 * CHUNKS,)),
            pltpu.SemaphoreType.DMA((1 + 3 * CHUNKS,)),
        ],
        compiler_params=pltpu.CompilerParams(vmem_limit_bytes=62 << 20),
    )(*results)


def solution(mesh):
    placed = (P("row", "col"), P("col", "row"), P("col", "row"), P("row", "col"), P("row", "col"))
    return jax.shard_map(
        on_device,
        mesh=mesh,
        in_specs=placed,
        out_specs=(P("row", "col"), P("col", "row"), P("col", "row"), P("row", "col")),
        check_vma=False,
    )
```

```python
import functools

import jax
import jax.numpy as jnp
from jax import lax
from jax.experimental import pallas as pl
from jax.experimental.pallas import tpu as pltpu
from jax.sharding import PartitionSpec as P

MESH = pl.DeviceIdType.MESH
F32, BF16 = jnp.float32, jnp.bfloat16
NY, NZ, NX, NC = 4, 16, 4, 2
TOK, HID, FEAT = 8, 256, 1024
LEFT, RIGHT = 640, 384
SLOTS = NZ // 2
GROUP = SLOTS * TOK // NC
ROWS = NY * SLOTS * TOK
WIDE = 3 * HID


def contract_cols(left, right):
    return lax.dot_general(left, right, (((1,), (1,)), ((), ())), preferred_element_type=F32)


def contract_rows(left, right):
    return lax.dot_general(left, right, (((0,), (0,)), ((), ())), preferred_element_type=F32)


def kernel(
    x_in, wg_in, wu_in, wd_in, dy_in,
    gi_out, gw_out, uw_out, dw_out,
    t, xm, dm, w2, wd,
    part, r1, s, s16, r2, hg,
    gs, yr, acc1, acc2, nb1, nra1, nrb1, nrc1, nb2, nra2, nrb2, nrc2, ty, tr, tot, cs, cr,
    gw2, dwd,
    send_sem, recv_sem, load_sem,
):
    row, col = lax.axis_index("row"), lax.axis_index("col")
    y, z = row // NZ, row % NZ
    x, c = col // NC, col % NC
    o = 1 - c

    places = {}

    def at(dy=0, dz=0, dx=0):
        if (dy, dz, dx) not in places:
            places[dy, dz, dx] = (
                ((y + dy + NY) % NY) * NZ + (z + dz + NZ) % NZ,
                ((x + dx + NX) % NX) * NC + c,
            )
        return places[dy, dz, dx]

    other = (row, x * NC + o)

    peers = [at(dz=k) for k in (3, -3)] + [at(dy=k) for k in (2, 1, -1)] + [at(dz=k) for k in (2, -2, 1, -1)]
    peers += [at(dx=k) for k in (2, 1, -1)] + [other]
    barrier = pltpu.get_barrier_semaphore()
    for peer in peers:
        pl.semaphore_signal(barrier, inc=1, device_id=peer, device_id_type=MESH)

    loads = []

    def load(src, dst):
        copy = pltpu.make_async_copy(src, dst, load_sem.at[len(loads)])
        copy.start()
        loads.append(copy)
        return copy

    at(dz=6), at(dz=-6)
    own = [load(x_in, t.at[0, 0, 0]), load(dy_in, t.at[1, 0, 0])]
    weights = [
        load(wg_in, w2.at[:, pl.ds(0, HID)]),
        load(wu_in, w2.at[:, pl.ds(HID, HID)]),
        load(wd_in, wd),
    ]

    for copy in own:
        copy.wait()
    pl.semaphore_wait(barrier, len(peers))

    sent = []

    def send(src, dst, to):
        i = len(sent)
        copy = pltpu.make_async_remote_copy(
            src_ref=src, dst_ref=dst, send_sem=send_sem.at[i], recv_sem=recv_sem.at[i],
            device_id=to, device_id_type=MESH,
        )
        copy.start()
        sent.append(copy)
        return copy

    def arrived(copies):
        for copy in copies:
            copy.wait_recv()

    def spread(which, slots):
        return [send(t.at[which, 0, slots], t.at[which, NY - k, slots], at(dy=k)) for k in (2, 1, 3)]

    def near(which, ys, start, size):
        def to(offset):
            return t.at[which, ys, pl.ds(offset + start, size)]

        return [send(to(0), to(5), at(dz=1)), send(to(0), to(10), at(dz=-1))]

    def near_last(which, ys):
        return near(which, ys, 3, 2) + [
            send(t.at[which, ys, pl.ds(3, 1)], t.at[which, ys, pl.ds(15, 1)], at(dz=-2))
        ]

    both, acts, grads = slice(None), 0, 1
    first, all_y = pl.ds(0, 1), slice(None)
    far = []
    for i, k in ((2, 3), (1, -3)):
        far.append(send(t.at[:, 0, 0], t.at[:, 0, i], at(dz=k)))
    near0 = near(acts, first, 0, 1)
    early0 = spread(both, pl.ds(0, 1))
    arrived(near0)
    late0 = spread(acts, pl.ds(5, 1))
    late1 = spread(acts, pl.ds(10, 1))
    arrived(far[:2])
    far += [send(t.at[:, 0, 2], t.at[:, 0, 4], at(dz=3)), send(t.at[:, 0, 1], t.at[:, 0, 3], at(dz=-3))]
    near1 = near(acts, first, 1, 2)
    early1 = spread(both, pl.ds(1, 2))
    arrived(early0)
    grad_near0 = near(grads, all_y, 0, 1)
    arrived(far[2:])
    near2 = near_last(acts, first)
    early2 = spread(both, pl.ds(3, 2))
    arrived(near1)
    late0 += spread(acts, pl.ds(6, 2))
    late1 += spread(acts, pl.ds(11, 2))
    arrived(early1)
    grad_near1 = near(grads, all_y, 1, 2)
    grad_near2 = near(grads, first, 3, 2)
    arrived(near2)
    late1 += spread(acts, pl.ds(8, 2)) + spread(acts, pl.ds(13, 3))
    arrived(early2)
    grad_near2 += near(grads, pl.ds(1, 3), 3, 2)
    grad_near2.append(send(t.at[grads, :, 3], t.at[grads, :, 15], at(dz=-2)))
    for copy in weights:
        copy.wait()

    def compact(src, dst, half):
        for i in range(2 * NY):
            slab = t[src, i // 2, pl.ds(half * SLOTS + i % 2 * 4, 4)].astype(F32).reshape(4 * TOK, FEAT)
            dst[pl.ds(half * ROWS + i * 4 * TOK, 4 * TOK), :] = slab.astype(BF16)

    def reduce_parts(half, of_grads):
        rows = pl.ds(half * ROWS, ROWS)
        pre_part, grad_part = pl.ds(0, 2 * HID), pl.ds(2 * HID, HID)
        compact(acts, xm, half)
        pre = jnp.dot(xm[rows, :], w2[...], preferred_element_type=F32)
        part[half, :, :, :, pre_part] = pre.reshape(NX, NC, GROUP, 2 * HID)
        to_other = [send(part.at[half, :, o, :, pre_part], r1.at[half, :, :, pre_part], other)]
        arrived(of_grads)
        compact(grads, dm, half)
        part[half, :, :, :, grad_part] = contract_cols(dm[rows, :], wd[...]).reshape(NX, NC, GROUP, HID)
        to_other.append(send(part.at[half, :, o, :, grad_part], r1.at[half, :, :, grad_part], other))
        arrived(to_other)
        over_x = []
        for k in (2, 1, 3, 0):
            m = (x + k) % NX
            value = part[half, m, c] + r1[half, m]
            if k:
                s16[half, k] = value.astype(BF16)
                over_x.append(send(s16.at[half, k], r2.at[half, k], at(dx=k)))
            else:
                s[half] = value
        return over_x

    grad_part, hid_part = pl.ds(0, 2 * HID), pl.ds(2 * HID, HID)

    def activate(half, over_x):
        arrived(over_x)
        total = s[half] + r2[half, 1].astype(F32) + r2[half, 2].astype(F32) + r2[half, 3].astype(F32)
        pre_gate, pre_up, grad_hidden = total[:, :HID], total[:, HID : 2 * HID], total[:, 2 * HID :]
        sigma = jax.nn.sigmoid(pre_gate)
        silu = pre_gate * sigma
        grad_gate = grad_hidden * pre_up * sigma * (1.0 + pre_gate * (1.0 - sigma))
        hg[half, x, c, :, pl.ds(0, HID)] = grad_gate.astype(BF16)
        hg[half, x, c, :, pl.ds(HID, HID)] = (grad_hidden * silu).astype(BF16)
        hg[half, x, c, :, pl.ds(2 * HID, HID)] = (silu * pre_up).astype(BF16)
        mine = hg.at[half, x, c]
        return [
            [send(mine.at[:, what], mine.at[:, what], at(dx=k)) for k in (2, 1, 3)] for what in (grad_part, hid_part)
        ]

    def pass_on(half, copies, what):
        mine = hg.at[half, x, c, :, what]
        crossed = [send(mine, mine, other)]
        for k, copy in zip((2, 1, 3), copies):
            arrived([copy])
            block = hg.at[half, (x - k + NX) % NX, c, :, what]
            crossed.append(send(block, block, other))
        return crossed

    arrived(late0)
    over_x0 = reduce_parts(0, grad_near0[:1] + grad_near1[:1])
    arrived(late1)
    over_x1 = reduce_parts(1, grad_near0[1:] + grad_near1[1:] + grad_near2)
    gathered0 = activate(0, over_x0)
    gathered1 = activate(1, over_x1)
    def input_grad(half, columns):
        product = contract_cols(hg[half, :, :, :, : 2 * HID].reshape(ROWS, 2 * HID), w2[columns, :])
        return product.reshape(NY, SLOTS, TOK, product.shape[-1])

    def send_near(block, a, b, c):
        return [send(block[0], a, at(dz=-1)), send(block[1], b, at(dz=1)), send(block[2], c, at(dz=2))]

    left_y, right_near = [], []
    for half, gathered in enumerate((gathered0, gathered1)):
        arrived(pass_on(half, gathered[0], grad_part))
        rows = pl.ds(half * SLOTS * TOK, SLOTS * TOK)
        grad = input_grad(half, slice(0, LEFT)).reshape(NY, SLOTS * TOK, LEFT)
        for k in (2, 1, 3):
            gs[k, rows] = grad[k].astype(BF16)
            left_y.append(send(gs.at[k, rows], yr.at[k, rows], at(dy=k)))
        acc1[rows, :] = grad[0]
        grad = input_grad(half, slice(LEFT, FEAT))
        if half == 0:
            acc2[...] = grad[:, :5]
            nb2[:, pl.ds(0, 3)] = grad[:, 5:].astype(BF16)
            right_near.append(send(nb2.at[:, pl.ds(0, 3)], nra2.at[:, pl.ds(0, 3)], at(dz=-1)))
        else:
            nb2[:, pl.ds(3, 8)] = grad.astype(BF16)
            right_near.append(send(nb2.at[:, pl.ds(5, 5)], nrb2, at(dz=1)))
            right_near.append(send(nb2.at[:, pl.ds(3, 2)], nra2.at[:, pl.ds(3, 2)], at(dz=-1)))
            right_near.append(send(nb2.at[:, pl.ds(10, 1)], nrc2, at(dz=2)))

    outs = []
    arrived(pass_on(0, gathered0[1], hid_part) + pass_on(1, gathered1[1], hid_part))
    dwd[...] = contract_rows(hg[:, :, :, :, 2 * HID :].reshape(2 * ROWS, HID), dm[...]).astype(BF16)
    outs.append(load(dwd, dw_out))
    gw2[...] = contract_rows(xm[...], hg[:, :, :, :, : 2 * HID].reshape(2 * ROWS, 2 * HID)).astype(BF16)
    outs.append(load(gw2.at[:, pl.ds(0, HID)], gw_out))
    outs.append(load(gw2.at[:, pl.ds(HID, HID)], uw_out))

    arrived(right_near)
    right_y = []
    for k in (2, 1, 3, 0):
        acc2[k] += nra2[k].astype(F32) + nrb2[k].astype(F32)
        acc2[k, 3] += nrc2[k, 0].astype(F32)
        if k:
            ty[k] = acc2[k].astype(BF16)
            right_y.append(send(ty.at[k], tr.at[k], at(dy=k)))

    arrived(left_y)
    total = acc1[...] + yr[1].astype(F32) + yr[2].astype(F32) + yr[3].astype(F32)
    acc1[...] = total
    nb1[...] = total[5 * TOK :].reshape(11, TOK, LEFT).astype(BF16)
    left_near = send_near([nb1.at[pl.ds(0, 5)], nb1.at[pl.ds(5, 5)], nb1.at[pl.ds(10, 1)]], nra1, nrb1, nrc1)
    left, right = pl.ds(0, LEFT), pl.ds(LEFT, RIGHT)
    arrived(right_y)
    tot[:, :, right] = acc2[0] + tr[1].astype(F32) + tr[2].astype(F32) + tr[3].astype(F32)
    arrived(left_near)
    tot[:, :, left] = acc1[: 5 * TOK].reshape(5, TOK, LEFT) + nra1[...].astype(F32) + nrb1[...].astype(F32)
    tot[3, :, left] += nrc1[0].astype(F32)

    far = []
    for i, k in ((3, 6), (4, -6), (1, 3), (2, -3)):
        cs[i] = tot[i].astype(BF16)
        far.append(send(cs.at[i], cr.at[i], at(dz=k)))
    arrived(far)
    gi_out[...] = tot[0] + cr[1].astype(F32) + cr[2].astype(F32) + cr[3].astype(F32) + cr[4].astype(F32)

    for copy in outs:
        copy.wait()
    for copy in sent:
        copy.wait_send()


def write_out(*refs):
    sources, results, (small, wide, load_sem, store_sem) = refs[:4], refs[4:8], refs[8:]
    pieces = [(sources[0], small, results[0])]
    for i in range(1, 4):
        rows = sources[i].shape[0] // CHUNKS
        for j in range(CHUNKS):
            piece = pl.ds(j * rows, rows)
            held = wide[i - 1].at[piece]
            pieces.append((sources[i].at[piece], held, results[i].at[piece]))
    loads = [pltpu.make_async_copy(a, b, load_sem.at[n]) for n, (a, b, _) in enumerate(pieces)]
    stores = [pltpu.make_async_copy(b, c, store_sem.at[n]) for n, (_, b, c) in enumerate(pieces)]
    for copy in loads:
        copy.start()
    for i, copy in enumerate(loads):
        copy.wait()
        stores[i].start()
    for copy in stores:
        copy.wait()


CHUNKS = 2
N_SENDS = 112
N_LOADS = 8


def on_device(activations, gate_weight, up_weight, down_weight, out_grad):
    anywhere = pl.BlockSpec(memory_space=pl.ANY)
    hbm = pl.BlockSpec(memory_space=pltpu.HBM)
    vmem = pl.BlockSpec(memory_space=pltpu.VMEM)
    results = pl.pallas_call(
        kernel,
        out_shape=(
            jax.ShapeDtypeStruct((TOK, FEAT), F32),
            jax.ShapeDtypeStruct((FEAT, HID), BF16),
            jax.ShapeDtypeStruct((FEAT, HID), BF16),
            jax.ShapeDtypeStruct((HID, FEAT), BF16),
        ),
        in_specs=[hbm] * 5,
        out_specs=(vmem, anywhere, anywhere, anywhere),
        scratch_shapes=[
            pltpu.VMEM((2, NY, NZ, TOK, FEAT), BF16),
            pltpu.VMEM((2 * ROWS, FEAT), BF16),
            pltpu.VMEM((2 * ROWS, FEAT), BF16),
            pltpu.VMEM((FEAT, 2 * HID), BF16),
            pltpu.VMEM((HID, FEAT), BF16),
            pltpu.VMEM((2, NX, NC, GROUP, WIDE), F32),
            pltpu.VMEM((2, NX, GROUP, WIDE), F32),
            pltpu.VMEM((2, GROUP, WIDE), F32),
            pltpu.VMEM((2, NX, GROUP, WIDE), BF16),
            pltpu.VMEM((2, NX, GROUP, WIDE), BF16),
            pltpu.VMEM((2, NX, NC, GROUP, WIDE), BF16),
            pltpu.VMEM((NY, NZ * TOK, LEFT), BF16),
            pltpu.VMEM((NY, NZ * TOK, LEFT), BF16),
            pltpu.VMEM((NZ * TOK, LEFT), F32),
            pltpu.VMEM((NY, 5, TOK, RIGHT), F32),
            pltpu.VMEM((11, TOK, LEFT), BF16),
            pltpu.VMEM((5, TOK, LEFT), BF16),
            pltpu.VMEM((5, TOK, LEFT), BF16),
            pltpu.VMEM((1, TOK, LEFT), BF16),
            pltpu.VMEM((NY, 11, TOK, RIGHT), BF16),
            pltpu.VMEM((NY, 5, TOK, RIGHT), BF16),
            pltpu.VMEM((NY, 5, TOK, RIGHT), BF16),
            pltpu.VMEM((NY, 1, TOK, RIGHT), BF16),
            pltpu.VMEM((NY, 5, TOK, RIGHT), BF16),
            pltpu.VMEM((NY, 5, TOK, RIGHT), BF16),
            pltpu.VMEM((5, TOK, FEAT), F32),
            pltpu.VMEM((5, TOK, FEAT), BF16),
            pltpu.VMEM((5, TOK, FEAT), BF16),
            pltpu.VMEM((FEAT, 2 * HID), BF16),
            pltpu.VMEM((HID, FEAT), BF16),
            pltpu.SemaphoreType.DMA((N_SENDS,)),
            pltpu.SemaphoreType.DMA((N_SENDS,)),
            pltpu.SemaphoreType.DMA((N_LOADS,)),
        ],
        compiler_params=pltpu.CompilerParams(
            collective_id=0, has_side_effects=True, vmem_limit_bytes=62 << 20
        ),
        cost_estimate=pl.CostEstimate(
            flops=16 * NY * NZ * TOK * FEAT * HID, bytes_accessed=12 * FEAT * HID, transcendentals=0
        ),
    )(activations, gate_weight, up_weight, down_weight, out_grad)
    return pl.pallas_call(
        write_out,
        out_shape=tuple(jax.ShapeDtypeStruct(r.shape, r.dtype) for r in results),
        in_specs=[hbm] * 4,
        out_specs=(hbm,) * 4,
        scratch_shapes=[
            pltpu.VMEM((TOK, FEAT), F32),
            [pltpu.VMEM(r.shape, BF16) for r in results[1:]],
            pltpu.SemaphoreType.DMA((1 + 3 * CHUNKS,)),
            pltpu.SemaphoreType.DMA((1 + 3 * CHUNKS,)),
        ],
        compiler_params=pltpu.CompilerParams(vmem_limit_bytes=62 << 20),
    )(*results)


def solution(mesh):
    placed = (P("row", "col"), P("col", "row"), P("col", "row"), P("row", "col"), P("row", "col"))
    return jax.shard_map(
        on_device,
        mesh=mesh,
        in_specs=placed,
        out_specs=(P("row", "col"), P("col", "row"), P("col", "row"), P("row", "col")),
        check_vma=False,
    )
```

```python
import functools

import jax
import jax.numpy as jnp
from jax import lax
from jax.experimental import pallas as pl
from jax.experimental.pallas import tpu as pltpu
from jax.sharding import PartitionSpec as P

MESH = pl.DeviceIdType.MESH
F32, BF16 = jnp.float32, jnp.bfloat16
NY, NZ, NX, NC = 4, 16, 4, 2
TOK, HID, FEAT = 8, 256, 1024
LEFT, RIGHT = 640, 384
SLOTS = NZ // 2
GROUP = SLOTS * TOK // NC
ROWS = NY * SLOTS * TOK
WIDE = 3 * HID


def contract_cols(left, right):
    return lax.dot_general(left, right, (((1,), (1,)), ((), ())), preferred_element_type=F32)


def contract_rows(left, right):
    return lax.dot_general(left, right, (((0,), (0,)), ((), ())), preferred_element_type=F32)


def kernel(
    x_in, wg_in, wu_in, wd_in, dy_in,
    gi_out, gw_out, uw_out, dw_out,
    t, xm, dm, w2, wd,
    part, r1, s, s16, r2, hg,
    gs, yr, acc1, acc2, nb1, nra1, nrb1, nrc1, nb2, nra2, nrb2, nrc2, ty, tr, tot, cs, cr,
    gw2, dwd,
    send_sem, recv_sem, load_sem,
):
    row, col = lax.axis_index("row"), lax.axis_index("col")
    y, z = row // NZ, row % NZ
    x, c = col // NC, col % NC
    o = 1 - c

    places = {}

    def at(dy=0, dz=0, dx=0):
        if (dy, dz, dx) not in places:
            places[dy, dz, dx] = (
                ((y + dy + NY) % NY) * NZ + (z + dz + NZ) % NZ,
                ((x + dx + NX) % NX) * NC + c,
            )
        return places[dy, dz, dx]

    other = (row, x * NC + o)

    peers = [at(dz=k) for k in (3, -3)] + [at(dy=k) for k in (2, 1, -1)] + [at(dz=k) for k in (1, -1)]
    peers += [at(dx=k) for k in (2, 1, -1)] + [other]
    barrier = pltpu.get_barrier_semaphore()
    for peer in peers:
        pl.semaphore_signal(barrier, inc=1, device_id=peer, device_id_type=MESH)

    loads = []

    def load(src, dst):
        copy = pltpu.make_async_copy(src, dst, load_sem.at[len(loads)])
        copy.start()
        loads.append(copy)
        return copy

    at(dz=6), at(dz=-6)
    own = [load(x_in, t.at[0, 0, 0]), load(dy_in, t.at[1, 0, 0])]
    weights = [
        load(wg_in, w2.at[:, pl.ds(0, HID)]),
        load(wu_in, w2.at[:, pl.ds(HID, HID)]),
        load(wd_in, wd),
    ]

    for copy in own:
        copy.wait()
    pl.semaphore_wait(barrier, len(peers))

    sent = []

    def send(src, dst, to):
        i = len(sent)
        copy = pltpu.make_async_remote_copy(
            src_ref=src, dst_ref=dst, send_sem=send_sem.at[i], recv_sem=recv_sem.at[i],
            device_id=to, device_id_type=MESH,
        )
        copy.start()
        sent.append(copy)
        return copy

    def arrived(copies):
        for copy in copies:
            copy.wait_recv()

    def spread(which, slots):
        return [send(t.at[which, 0, slots], t.at[which, NY - k, slots], at(dy=k)) for k in (2, 1, 3)]

    def near(which, ys, start, size):
        def to(offset):
            return t.at[which, ys, pl.ds(offset + start, size)]

        return [send(to(0), to(5), at(dz=1)), send(to(0), to(10), at(dz=-1))]

    def near_last(which, ys):
        return near(which, ys, 3, 2) + [
            send(t.at[which, ys, pl.ds(3, 1)], t.at[which, ys, pl.ds(15, 1)], at(dz=-2))
        ]

    both, acts, grads = slice(None), 0, 1
    first, all_y = pl.ds(0, 1), slice(None)
    far = []
    for i, k in ((2, 3), (1, -3)):
        far.append(send(t.at[:, 0, 0], t.at[:, 0, i], at(dz=k)))
    near0 = near(acts, first, 0, 1)
    early0 = spread(both, pl.ds(0, 1))
    arrived(near0)
    late0 = spread(acts, pl.ds(5, 1))
    late1 = spread(acts, pl.ds(10, 1))
    arrived(far[:2])
    far += [send(t.at[:, 0, 2], t.at[:, 0, 4], at(dz=3)), send(t.at[:, 0, 1], t.at[:, 0, 3], at(dz=-3))]
    near1 = near(acts, first, 1, 2)
    early1 = spread(both, pl.ds(1, 2))
    arrived(early0)
    grad_near0 = near(grads, all_y, 0, 1)
    arrived(far[2:])
    near2 = near(acts, first, 3, 2)
    early2 = spread(both, pl.ds(3, 2))
    arrived(near1)
    near2.append(send(t.at[acts, first, pl.ds(3, 1)], t.at[acts, first, pl.ds(15, 1)], at(dz=-2)))
    late0 += spread(acts, pl.ds(6, 2))
    late1 += spread(acts, pl.ds(11, 2))
    arrived(early1)
    grad_near1 = near(grads, all_y, 1, 2)
    grad_near2 = near(grads, first, 3, 2)
    arrived(near2)
    late1 += spread(acts, pl.ds(8, 2)) + spread(acts, pl.ds(13, 3))
    arrived(early2)
    grad_near2 += near(grads, pl.ds(1, 3), 3, 2)
    grad_near2.append(send(t.at[grads, :, 3], t.at[grads, :, 15], at(dz=-2)))
    for copy in weights:
        copy.wait()

    def compact(src, dst, half):
        for i in range(2 * NY):
            slab = t[src, i // 2, pl.ds(half * SLOTS + i % 2 * 4, 4)].astype(F32).reshape(4 * TOK, FEAT)
            dst[pl.ds(half * ROWS + i * 4 * TOK, 4 * TOK), :] = slab.astype(BF16)

    def reduce_parts(half, of_grads):
        rows = pl.ds(half * ROWS, ROWS)
        pre_part, grad_part = pl.ds(0, 2 * HID), pl.ds(2 * HID, HID)
        compact(acts, xm, half)
        pre = jnp.dot(xm[rows, :], w2[...], preferred_element_type=F32)
        part[half, :, :, :, pre_part] = pre.reshape(NX, NC, GROUP, 2 * HID)
        to_other = [send(part.at[half, :, o, :, pre_part], r1.at[half, :, :, pre_part], other)]
        arrived(of_grads)
        compact(grads, dm, half)
        part[half, :, :, :, grad_part] = contract_cols(dm[rows, :], wd[...]).reshape(NX, NC, GROUP, HID)
        to_other.append(send(part.at[half, :, o, :, grad_part], r1.at[half, :, :, grad_part], other))
        arrived(to_other)
        over_x = []
        for k in (2, 1, 3, 0):
            m = (x + k) % NX
            value = part[half, m, c] + r1[half, m]
            if k:
                s16[half, k] = value.astype(BF16)
                over_x.append(send(s16.at[half, k], r2.at[half, k], at(dx=k)))
            else:
                s[half] = value
        return over_x

    grad_part, hid_part = pl.ds(0, 2 * HID), pl.ds(2 * HID, HID)

    def activate(half, over_x):
        arrived(over_x)
        total = s[half] + r2[half, 1].astype(F32) + r2[half, 2].astype(F32) + r2[half, 3].astype(F32)
        pre_gate, pre_up, grad_hidden = total[:, :HID], total[:, HID : 2 * HID], total[:, 2 * HID :]
        sigma = jax.nn.sigmoid(pre_gate)
        silu = pre_gate * sigma
        grad_gate = grad_hidden * pre_up * sigma * (1.0 + pre_gate * (1.0 - sigma))
        hg[half, x, c, :, pl.ds(0, HID)] = grad_gate.astype(BF16)
        hg[half, x, c, :, pl.ds(HID, HID)] = (grad_hidden * silu).astype(BF16)
        hg[half, x, c, :, pl.ds(2 * HID, HID)] = (silu * pre_up).astype(BF16)
        mine = hg.at[half, x, c]
        return [
            [send(mine.at[:, what], mine.at[:, what], at(dx=k)) for k in (2, 1, 3)] for what in (grad_part, hid_part)
        ]

    def pass_on(half, copies, what):
        mine = hg.at[half, x, c, :, what]
        crossed = [send(mine, mine, other)]
        for k, copy in zip((2, 1, 3), copies):
            arrived([copy])
            block = hg.at[half, (x - k + NX) % NX, c, :, what]
            crossed.append(send(block, block, other))
        return crossed

    arrived(late0)
    over_x0 = reduce_parts(0, grad_near0[:1] + grad_near1[:1])
    arrived(late1)
    over_x1 = reduce_parts(1, grad_near0[1:] + grad_near1[1:] + grad_near2)
    gathered0 = activate(0, over_x0)
    gathered1 = activate(1, over_x1)
    def input_grad(half, columns):
        product = contract_cols(hg[half, :, :, :, : 2 * HID].reshape(ROWS, 2 * HID), w2[columns, :])
        return product.reshape(NY, SLOTS, TOK, product.shape[-1])

    def send_near(block, a, b, c):
        return [send(block[0], a, at(dz=-1)), send(block[1], b, at(dz=1)), send(block[2], c, at(dz=2))]

    left_y, right_near = [], []
    for half, gathered in enumerate((gathered0, gathered1)):
        arrived(pass_on(half, gathered[0], grad_part))
        rows = pl.ds(half * SLOTS * TOK, SLOTS * TOK)
        grad = input_grad(half, slice(0, LEFT)).reshape(NY, SLOTS * TOK, LEFT)
        for k in (2, 1, 3):
            gs[k, rows] = grad[k].astype(BF16)
            left_y.append(send(gs.at[k, rows], yr.at[k, rows], at(dy=k)))
        acc1[rows, :] = grad[0]
        grad = input_grad(half, slice(LEFT, FEAT))
        if half == 0:
            acc2[...] = grad[:, :5]
            nb2[:, pl.ds(0, 3)] = grad[:, 5:].astype(BF16)
            right_near.append(send(nb2.at[:, pl.ds(0, 3)], nra2.at[:, pl.ds(0, 3)], at(dz=-1)))
        else:
            nb2[:, pl.ds(3, 8)] = grad.astype(BF16)
            right_near.append(send(nb2.at[:, pl.ds(5, 5)], nrb2, at(dz=1)))
            right_near.append(send(nb2.at[:, pl.ds(3, 2)], nra2.at[:, pl.ds(3, 2)], at(dz=-1)))
            right_near.append(send(nb2.at[:, pl.ds(10, 1)], nrc2, at(dz=2)))

    outs = []
    arrived(pass_on(0, gathered0[1], hid_part) + pass_on(1, gathered1[1], hid_part))
    dwd[...] = contract_rows(hg[:, :, :, :, 2 * HID :].reshape(2 * ROWS, HID), dm[...]).astype(BF16)
    outs.append(load(dwd, dw_out))
    gw2[...] = contract_rows(xm[...], hg[:, :, :, :, : 2 * HID].reshape(2 * ROWS, 2 * HID)).astype(BF16)
    outs.append(load(gw2.at[:, pl.ds(0, HID)], gw_out))
    outs.append(load(gw2.at[:, pl.ds(HID, HID)], uw_out))

    arrived(right_near)
    right_y = []
    for k in (2, 1, 3, 0):
        acc2[k] += nra2[k].astype(F32) + nrb2[k].astype(F32)
        acc2[k, 3] += nrc2[k, 0].astype(F32)
        if k:
            ty[k] = acc2[k].astype(BF16)
            right_y.append(send(ty.at[k], tr.at[k], at(dy=k)))

    arrived(left_y)
    total = acc1[...] + yr[1].astype(F32) + yr[2].astype(F32) + yr[3].astype(F32)
    acc1[...] = total
    nb1[...] = total[5 * TOK :].reshape(11, TOK, LEFT).astype(BF16)
    left_near = send_near([nb1.at[pl.ds(0, 5)], nb1.at[pl.ds(5, 5)], nb1.at[pl.ds(10, 1)]], nra1, nrb1, nrc1)
    left, right = pl.ds(0, LEFT), pl.ds(LEFT, RIGHT)
    arrived(right_y)
    tot[:, :, right] = acc2[0] + tr[1].astype(F32) + tr[2].astype(F32) + tr[3].astype(F32)
    arrived(left_near)
    tot[:, :, left] = acc1[: 5 * TOK].reshape(5, TOK, LEFT) + nra1[...].astype(F32) + nrb1[...].astype(F32)
    tot[3, :, left] += nrc1[0].astype(F32)

    far = []
    for i, k in ((3, 6), (4, -6), (1, 3), (2, -3)):
        cs[i] = tot[i].astype(BF16)
        far.append(send(cs.at[i], cr.at[i], at(dz=k)))
    arrived(far)
    gi_out[...] = tot[0] + cr[1].astype(F32) + cr[2].astype(F32) + cr[3].astype(F32) + cr[4].astype(F32)

    for copy in outs:
        copy.wait()
    for copy in sent:
        copy.wait_send()


def write_out(*refs):
    sources, results, (small, wide, load_sem, store_sem) = refs[:4], refs[4:8], refs[8:]
    pieces = [(sources[0], small, results[0])]
    for i in range(1, 4):
        rows = sources[i].shape[0] // CHUNKS
        for j in range(CHUNKS):
            piece = pl.ds(j * rows, rows)
            held = wide[i - 1].at[piece]
            pieces.append((sources[i].at[piece], held, results[i].at[piece]))
    loads = [pltpu.make_async_copy(a, b, load_sem.at[n]) for n, (a, b, _) in enumerate(pieces)]
    stores = [pltpu.make_async_copy(b, c, store_sem.at[n]) for n, (_, b, c) in enumerate(pieces)]
    for copy in loads:
        copy.start()
    for i, copy in enumerate(loads):
        copy.wait()
        stores[i].start()
    for copy in stores:
        copy.wait()


CHUNKS = 2
N_SENDS = 112
N_LOADS = 8


def on_device(activations, gate_weight, up_weight, down_weight, out_grad):
    anywhere = pl.BlockSpec(memory_space=pl.ANY)
    hbm = pl.BlockSpec(memory_space=pltpu.HBM)
    vmem = pl.BlockSpec(memory_space=pltpu.VMEM)
    results = pl.pallas_call(
        kernel,
        out_shape=(
            jax.ShapeDtypeStruct((TOK, FEAT), F32),
            jax.ShapeDtypeStruct((FEAT, HID), BF16),
            jax.ShapeDtypeStruct((FEAT, HID), BF16),
            jax.ShapeDtypeStruct((HID, FEAT), BF16),
        ),
        in_specs=[hbm] * 5,
        out_specs=(vmem, anywhere, anywhere, anywhere),
        scratch_shapes=[
            pltpu.VMEM((2, NY, NZ, TOK, FEAT), BF16),
            pltpu.VMEM((2 * ROWS, FEAT), BF16),
            pltpu.VMEM((2 * ROWS, FEAT), BF16),
            pltpu.VMEM((FEAT, 2 * HID), BF16),
            pltpu.VMEM((HID, FEAT), BF16),
            pltpu.VMEM((2, NX, NC, GROUP, WIDE), F32),
            pltpu.VMEM((2, NX, GROUP, WIDE), F32),
            pltpu.VMEM((2, GROUP, WIDE), F32),
            pltpu.VMEM((2, NX, GROUP, WIDE), BF16),
            pltpu.VMEM((2, NX, GROUP, WIDE), BF16),
            pltpu.VMEM((2, NX, NC, GROUP, WIDE), BF16),
            pltpu.VMEM((NY, NZ * TOK, LEFT), BF16),
            pltpu.VMEM((NY, NZ * TOK, LEFT), BF16),
            pltpu.VMEM((NZ * TOK, LEFT), F32),
            pltpu.VMEM((NY, 5, TOK, RIGHT), F32),
            pltpu.VMEM((11, TOK, LEFT), BF16),
            pltpu.VMEM((5, TOK, LEFT), BF16),
            pltpu.VMEM((5, TOK, LEFT), BF16),
            pltpu.VMEM((1, TOK, LEFT), BF16),
            pltpu.VMEM((NY, 11, TOK, RIGHT), BF16),
            pltpu.VMEM((NY, 5, TOK, RIGHT), BF16),
            pltpu.VMEM((NY, 5, TOK, RIGHT), BF16),
            pltpu.VMEM((NY, 1, TOK, RIGHT), BF16),
            pltpu.VMEM((NY, 5, TOK, RIGHT), BF16),
            pltpu.VMEM((NY, 5, TOK, RIGHT), BF16),
            pltpu.VMEM((5, TOK, FEAT), F32),
            pltpu.VMEM((5, TOK, FEAT), BF16),
            pltpu.VMEM((5, TOK, FEAT), BF16),
            pltpu.VMEM((FEAT, 2 * HID), BF16),
            pltpu.VMEM((HID, FEAT), BF16),
            pltpu.SemaphoreType.DMA((N_SENDS,)),
            pltpu.SemaphoreType.DMA((N_SENDS,)),
            pltpu.SemaphoreType.DMA((N_LOADS,)),
        ],
        compiler_params=pltpu.CompilerParams(
            collective_id=0, has_side_effects=True, vmem_limit_bytes=62 << 20
        ),
        cost_estimate=pl.CostEstimate(
            flops=16 * NY * NZ * TOK * FEAT * HID, bytes_accessed=12 * FEAT * HID, transcendentals=0
        ),
    )(activations, gate_weight, up_weight, down_weight, out_grad)
    return pl.pallas_call(
        write_out,
        out_shape=tuple(jax.ShapeDtypeStruct(r.shape, r.dtype) for r in results),
        in_specs=[hbm] * 4,
        out_specs=(hbm,) * 4,
        scratch_shapes=[
            pltpu.VMEM((TOK, FEAT), F32),
            [pltpu.VMEM(r.shape, BF16) for r in results[1:]],
            pltpu.SemaphoreType.DMA((1 + 3 * CHUNKS,)),
            pltpu.SemaphoreType.DMA((1 + 3 * CHUNKS,)),
        ],
        compiler_params=pltpu.CompilerParams(vmem_limit_bytes=62 << 20),
    )(*results)


def solution(mesh):
    placed = (P("row", "col"), P("col", "row"), P("col", "row"), P("row", "col"), P("row", "col"))
    return jax.shard_map(
        on_device,
        mesh=mesh,
        in_specs=placed,
        out_specs=(P("row", "col"), P("col", "row"), P("col", "row"), P("row", "col")),
        check_vma=False,
    )
```
